512 devices in a mesh: row: 8 (over x, z_hi), col: 8 (over y, core), dp: 8 (over z_lo).
Axes of the slice: x: 4, y: 4, z: 16 (z_hi: 2, z_lo: 8; z = z_hi * 8 + z_lo), core: 2. Of those that a mesh axis runs over, the one named last changes fastest.
Arguments:
- inputs: bfloat16 [8, 256, 4096], P('dp', 'col', 'row'), may hold values from -6 to 6
- w_gate: bfloat16 [4096, 14336], P('row', 'col'), may hold values from -0.09375 to 0.09375
- w_up: bfloat16 [4096, 14336], P('row', 'col'), may hold values from -0.09375 to 0.09375
- cotangent: bfloat16 [8, 256, 14336], P('dp', 'row', 'col'), may hold values from -6 to 6
Outputs:
- hidden: bfloat16 [8, 256, 14336], P('dp', 'row', 'col')
- grad_inputs: bfloat16 [8, 256, 4096], P('dp', 'col', 'row')
- grad_gate: bfloat16 [4096, 14336], P('row', ('col', 'dp'))
- grad_up: bfloat16 [4096, 14336], P('row', ('col', 'dp'))
The draws below stay inside these ranges and needn't reach their ends.
All inputs are finite; a program needn't handle non-finite values.
Results may differ from the reference program's by a relative error of at most 0.028.
Values may be sent and summed in bfloat16 or wider, within the bound.
A program may use at most 64 MiB of HBM per device.

```python
import jax
import jax.numpy as jnp
from jax import lax

D = 4096
FF = 14336
TOK = 256
N_COL = 8
N_DP = 8


def spiked(values, stream_key, source, target, blocks, factor):
    def block_of(dim):
        return (jnp.arange(values.shape[dim]) // (values.shape[dim] // blocks)).reshape((-1,) + (1,) * (values.ndim - 1 - dim))

    one_side = jax.random.permutation(stream_key, blocks)[block_of(target)]
    second = (block_of(target) + blocks // 2) % blocks
    return jnp.where((block_of(source) == one_side) | (block_of(source) == second), factor * values, values)


def levels(stream_key, shape, pieces, low, high):
    gain = 1.0
    for axis_at, parts in pieces:
        heights = jax.random.uniform(jax.random.fold_in(jax.random.fold_in(stream_key, 6), axis_at), (parts,), jnp.float32, low / len(pieces), high / len(pieces))
        gain = gain * jnp.repeat(jnp.exp(heights), shape[axis_at] // parts).reshape((-1,) + (1,) * (len(shape) - 1 - axis_at))
    return gain


def normal_values(stream_key, shape, scale, reach, split=(), held_as=jnp.bfloat16):
    entries = scale * jax.random.normal(stream_key, shape, jnp.float32)
    if split:
        entries = entries * levels(stream_key, shape, split, -0.22, 0.18)
    return jnp.clip(entries, -reach, reach).astype(held_as)


def heavy_noise(key, shape, spread, limit, pieces, heavy, dtype=jnp.bfloat16):
    array = spread * jax.random.normal(key, shape, jnp.float32)
    if pieces:
        array = array * levels(key, shape, pieces, -0.22, 0.18)
    return jnp.clip(spiked(array, jax.random.fold_in(key, 3), *heavy), -limit, limit).astype(dtype)


def setup_inputs(seed: int = 0) -> dict:
    splits = jax.random.split(jax.random.key(seed), 5)
    return {
        "inputs": heavy_noise(splits[0], (N_DP, TOK, D), 1.0, 6.0, ((0, 8), (1, 8), (2, 8)), (2, 1, 8, 2.0)),
        "w_gate": normal_values(splits[1], (D, FF), D ** -0.5, 0.09375, ((0, 8), (1, 8))),
        "w_up": normal_values(splits[2], (D, FF), D ** -0.5, 0.09375, ((0, 8), (1, 8))),
        "cotangent": normal_values(splits[3], (N_DP, TOK, FF), 1.0, 6.0, ((0, 8), (1, 8), (2, 8))),
    }


def reference(inputs, w_gate, w_up, cotangent):
    flat = inputs.reshape(N_DP * TOK, D)
    gate = jnp.dot(flat, w_gate, preferred_element_type=jnp.float32)
    upper = jnp.dot(flat, w_up, preferred_element_type=jnp.float32)
    sig = jax.nn.sigmoid(gate)
    act = gate * sig
    hidden = (act * upper).astype(jnp.bfloat16)
    slope = cotangent.reshape(N_DP * TOK, FF).astype(jnp.float32)
    d_gate = (slope * upper * sig * (1.0 + gate * (1.0 - sig))).astype(jnp.bfloat16)
    d_up = (slope * act).astype(jnp.bfloat16)
    width = FF // N_COL
    dims = (((1,), (1,)), ((), ()))
    total = jnp.zeros((N_DP * TOK, D), jnp.float32)
    for block in range(N_COL):
        lower = block * width
        upper_end = lower + width
        term = lax.dot_general(d_gate[:, lower:upper_end], w_gate[:, lower:upper_end], dims, preferred_element_type=jnp.float32)
        term = term + lax.dot_general(d_up[:, lower:upper_end], w_up[:, lower:upper_end], dims, preferred_element_type=jnp.float32)
        rounded = lax.optimization_barrier(term.astype(jnp.bfloat16))
        total = total + rounded.astype(jnp.float32)
    grad_inputs = total.astype(jnp.bfloat16).reshape(N_DP, TOK, D)
    tdims = (((0,), (0,)), ((), ()))
    sum_gate = jnp.zeros((D, FF), jnp.float32)
    sum_up = jnp.zeros((D, FF), jnp.float32)
    for replica in range(N_DP):
        lower = replica * TOK
        rows = flat[lower:lower + TOK]
        part_gate = lax.dot_general(rows, d_gate[lower:lower + TOK], tdims, preferred_element_type=jnp.float32)
        part_up = lax.dot_general(rows, d_up[lower:lower + TOK], tdims, preferred_element_type=jnp.float32)
        part_gate = lax.optimization_barrier(part_gate.astype(jnp.bfloat16))
        part_up = lax.optimization_barrier(part_up.astype(jnp.bfloat16))
        sum_gate = sum_gate + part_gate.astype(jnp.float32)
        sum_up = sum_up + part_up.astype(jnp.float32)
    return hidden.reshape(N_DP, TOK, FF), grad_inputs, sum_gate.astype(jnp.bfloat16), sum_up.astype(jnp.bfloat16)
```

```python
import functools

import jax
import jax.numpy as jnp
from jax import lax
from jax.experimental import pallas as pl
from jax.experimental.pallas import tpu as pltpu
from jax.sharding import PartitionSpec as P

MESH = pl.DeviceIdType.MESH
F32 = jnp.float32
BF16 = jnp.bfloat16


def wait_bytes(ref, sem):
    pltpu.make_async_copy(ref, ref, sem).wait()


def kernel(
    nx, ncol, nd, sub, pad, tb,
    in_ref, wg_ref, wu_ref, cot_ref,
    hid_ref, gi_ref, gg_ref, gu_ref,
    wg, wu, cot, wp, cotp, hidp, everyone, xsend, xrecv, zown, zsend, zrecv, dsend, dall, gsend, grecv, fsend, frecv, acc, giown,
    loc, agc_s, agc_r, agz_s, agz_r, agy_s, agy_r, x_s, x_r, z_s, z_r, dz_s, dz_r, dx_s, dx_r, g_s, g_r, f_s, f_r,
):
    row, col, d = lax.axis_index("row"), lax.axis_index("col"), lax.axis_index("dp")
    x, h = row // 2, row % 2
    nz = 2 * nd
    z = h * nd + d
    feat = wg.shape[0]

    def zdev(z2):
        return (x * 2 + z2 // nd, col, z2 % nd)

    def xdev(i):
        return (lax.rem(x + i, nx) * 2 + h, col, d)

    def cdev(i):
        return (row, lax.rem(col + i, ncol), d)

    def send(src, dst, ssem, rsem, dev):
        pltpu.make_async_remote_copy(
            src_ref=src, dst_ref=dst, send_sem=ssem, recv_sem=rsem, device_id=dev, device_id_type=MESH
        ).start()

    barrier = pltpu.get_barrier_semaphore()
    for i in range(1, ncol):
        pl.semaphore_signal(barrier, inc=1, device_id=cdev(i), device_id_type=MESH)
    for i in range(1, nx):
        pl.semaphore_signal(barrier, inc=1, device_id=xdev(i), device_id_type=MESH)
    for i in range(1, nz):
        pl.semaphore_signal(barrier, inc=1, device_id=zdev(lax.rem(z + i, nz)), device_id_type=MESH)
    loads = [
        pltpu.make_async_copy(wg_ref, wg, loc.at[0]),
        pltpu.make_async_copy(wu_ref, wu, loc.at[1]),
        pltpu.make_async_copy(cot_ref.at[0], cot, loc.at[2]),
        pltpu.make_async_copy(in_ref.at[0], everyone.at[0, pl.ds(col * tb, tb)], loc.at[3]),
    ]
    for load in loads:
        load.start()
    pl.semaphore_wait(barrier, ncol - 1 + nx - 1 + nz - 1)

    for i in range(1, ncol):
        send(in_ref.at[0], everyone.at[0, pl.ds(col * tb, tb)], agc_s, agc_r, cdev(i))
    for i in range(1, nd):
        send(in_ref.at[0], everyone.at[i, pl.ds(col * tb, tb)], agz_s, agz_r.at[i], (row, col, lax.rem(d + i, nd)))

    for load in loads:
        load.wait()

    @pl.loop(0, feat // 64)
    def _(q):
        rows = pl.ds(pl.multiple_of(q * 64, 64), 64)
        for j in range(nd):
            for k, w in enumerate((wg, wu)):
                wp[j, rows, k * pad : k * pad + sub] = w[rows, j * sub : (j + 1) * sub]
                wp[j, rows, k * pad + sub : (k + 1) * pad] = jnp.zeros((64, pad - sub), BF16)

    for j in range(nd):
        cotp[j, :, :sub] = cot[:, j * sub : (j + 1) * sub]
        cotp[j, :, sub:] = jnp.zeros((tb, pad - sub), BF16)
    acc[...] = jnp.zeros_like(acc)
    wait_bytes(everyone.at[0, pl.ds(0, (ncol - 1) * tb)], agc_r)

    two = 2 * tb

    def stage_a(s):
        j = lax.rem(d + s, nd)
        part = jnp.dot(everyone[0], wp[j], preferred_element_type=F32)
        xsend[s] = part.astype(BF16)
        for i in range(1, nx):
            other = lax.rem(x + i, nx)
            send(xsend.at[s, pl.ds(other * two, two)], xrecv.at[s, i - 1], x_s, x_r.at[s], xdev(i))

    def stage_y(s):
        mine = everyone.at[s, pl.ds(col * tb, tb)]
        wait_bytes(mine, agz_r.at[s])
        for i in range(1, ncol):
            send(mine, mine, agy_s, agy_r.at[s], cdev(i))

    def stage_b(s):
        wait_bytes(xrecv.at[s], x_r.at[s])

        def total(half):
            out = xsend[s, pl.ds(x * two + half * tb, tb)].astype(F32)
            for i in range(nx - 1):
                out = out + xrecv[s, i, pl.ds(half * tb, tb)].astype(F32)
            return out

        zsend[s] = total(1 - h).astype(BF16)
        send(zsend.at[s], zrecv.at[s], z_s, z_r.at[s], zdev(lax.rem(z + nd, nz)))
        zown[s] = total(h)

    def stage_c(s):
        j = lax.rem(d + s, nd)
        wait_bytes(zrecv.at[s], z_r.at[s])
        both = zown[s] + zrecv[s].astype(F32)
        gate, upper = both[:, :pad], both[:, pad:]
        sig = jax.nn.sigmoid(gate)
        act = gate * sig
        slope = cotp[j].astype(F32)
        hidp[j] = (act * upper).astype(BF16)
        dsend[s, :, :pad] = (slope * upper * sig * (1.0 + gate * (1.0 - sig))).astype(BF16)
        dsend[s, :, pad:] = (slope * act).astype(BF16)
        there = dall.at[s, pl.ds(row * tb, tb)]

        @pl.when(s == 0)
        def _():
            dall[0, pl.ds(row * tb, tb)] = dsend[0]
            send(dsend.at[0], there, dz_s, dz_r.at[s], (x * 2 + 1 - h, col, d))

        @pl.when(s > 0)
        def _():
            send(dsend.at[s], there, dz_s, dz_r.at[s], (x * 2, col, j))
            send(dsend.at[s], there, dz_s, dz_r.at[s], (x * 2 + 1, col, j))

    def stage_d(s):
        @pl.when(s == 0)
        def _():
            wait_bytes(dall.at[0, pl.ds(0, tb)], dz_r.at[0])

        @pl.when(s > 0)
        def _():
            wait_bytes(dall.at[s, pl.ds(0, two)], dz_r.at[s])

        mine = dall.at[s, pl.ds(x * two, two)]
        for i in range(1, nx):
            send(mine, mine, dx_s, dx_r.at[s], xdev(i))

    def stage_e(s):
        wait_bytes(dall.at[s, pl.ds(0, (nx - 1) * two)], dx_r.at[s])
        part = lax.dot_general(dall[s], wp[d], (((1,), (1,)), ((), ())), preferred_element_type=F32)
        gsend[s] = part.astype(BF16)
        for i in range(1, ncol):
            other = lax.rem(col + i, ncol)
            send(gsend.at[s, pl.ds(other * tb, tb)], grecv.at[s, i - 1], g_s, g_r.at[s], cdev(i))

        @pl.when(s > 0)
        def _():
            wait_bytes(everyone.at[s, pl.ds(0, (ncol - 1) * tb)], agy_r.at[s])

        acc[...] += lax.dot_general(everyone[s], dall[s], (((0,), (0,)), ((), ())), preferred_element_type=F32)

    def stage_f(s):
        wait_bytes(grecv.at[s], g_r.at[s])
        out = gsend[s, pl.ds(col * tb, tb)].astype(F32)
        for i in range(ncol - 1):
            out = out + grecv[s, i].astype(F32)

        @pl.when(s == 0)
        def _():
            giown[...] = out

        @pl.when(s > 0)
        def _():
            fsend[s] = out.astype(BF16)
            send(fsend.at[s], frecv.at[s], f_s, f_r.at[s], (row, col, lax.rem(d - s + nd, nd)))

    stages = ((stage_a, 0, 0), (stage_b, 1, 0), (stage_y, 0, 1), (stage_c, 3, 0), (stage_d, 5, 0), (stage_e, 6, 0), (stage_f, 7, 0))
    steps = nd + 7

    def body(t, carry):
        for fn, lag, first in stages:
            s = t - lag

            @pl.when((s >= first) & (s < nd))
            def _(fn=fn, s=s):
                fn(s)

        return carry

    lax.fori_loop(0, steps, body, None)

    for j in range(nd):
        hid_ref[0, :, j * sub : (j + 1) * sub] = hidp[j, :, :sub]
    gg_ref[...] = acc[:, :sub].astype(BF16)
    gu_ref[...] = acc[:, pad : pad + sub].astype(BF16)
    out = giown[...]
    for s in range(1, nd):
        wait_bytes(frecv.at[s], f_r.at[s])
        out = out + frecv[s].astype(F32)
    gi_ref[0] = out.astype(BF16)

    wait_bytes(everyone.at[0, pl.ds(0, (ncol - 1) * tb)], agc_s)
    wait_bytes(everyone.at[0, pl.ds(0, (nd - 1) * tb)], agz_s)
    wait_bytes(everyone.at[pl.ds(0, nd - 1), pl.ds(0, (ncol - 1) * tb)], agy_s)
    wait_bytes(xsend.at[:, pl.ds(0, (nx - 1) * two)], x_s)
    wait_bytes(zsend, z_s)
    wait_bytes(dsend, dz_s)
    wait_bytes(dsend.at[pl.ds(0, nd - 1)], dz_s)
    wait_bytes(dall.at[:, pl.ds(0, (nx - 1) * two)], dx_s)
    wait_bytes(gsend.at[:, pl.ds(0, (ncol - 1) * tb)], g_s)
    wait_bytes(fsend.at[pl.ds(0, nd - 1)], f_s)


def local(nx, ncol, nd, inputs, w_gate, w_up, cotangent):
    tb, feat = inputs.shape[1], inputs.shape[2]
    ff = w_gate.shape[1]
    sub = ff // nd
    pad = -(-sub // 128) * 128
    wide = 2 * pad
    tok = tb * ncol
    dma = pltpu.SemaphoreType.DMA
    any_spec = pl.BlockSpec(memory_space=pl.ANY)
    vmem = pl.BlockSpec(memory_space=pltpu.VMEM)
    return pl.pallas_call(
        functools.partial(kernel, nx, ncol, nd, sub, pad, tb),
        name="swiglu",
        out_shape=(
            jax.ShapeDtypeStruct((1, tb, ff), BF16),
            jax.ShapeDtypeStruct((1, tb, feat), BF16),
            jax.ShapeDtypeStruct((feat, sub), BF16),
            jax.ShapeDtypeStruct((feat, sub), BF16),
        ),
        in_specs=[any_spec] * 4,
        out_specs=(vmem,) * 4,
        scratch_shapes=[
            pltpu.VMEM((feat, ff), BF16),
            pltpu.VMEM((feat, ff), BF16),
            pltpu.VMEM((tb, ff), BF16),
            pltpu.VMEM((nd, feat, wide), BF16),
            pltpu.VMEM((nd, tb, pad), BF16),
            pltpu.VMEM((nd, tb, pad), BF16),
            pltpu.VMEM((nd, tok, feat), BF16),
            pltpu.VMEM((nd, tok, wide), BF16),
            pltpu.VMEM((nd, nx - 1, 2 * tb, wide), BF16),
            pltpu.VMEM((nd, tb, wide), F32),
            pltpu.VMEM((nd, tb, wide), BF16),
            pltpu.VMEM((nd, tb, wide), BF16),
            pltpu.VMEM((nd, tb, wide), BF16),
            pltpu.VMEM((nd, tok, wide), BF16),
            pltpu.VMEM((nd, tok, feat), BF16),
            pltpu.VMEM((nd, ncol - 1, tb, feat), BF16),
            pltpu.VMEM((nd, tb, feat), BF16),
            pltpu.VMEM((nd, tb, feat), BF16),
            pltpu.VMEM((feat, wide), F32),
            pltpu.VMEM((tb, feat), F32),
            dma((4,)),
            dma, dma,
            dma, dma((nd,)),
            dma, dma((nd,)),
            dma, dma((nd,)),
            dma, dma((nd,)),
            dma, dma((nd,)),
            dma, dma((nd,)),
            dma, dma((nd,)),
            dma, dma((nd,)),
        ],
        compiler_params=pltpu.CompilerParams(
            collective_id=0, has_side_effects=True, vmem_limit_bytes=50 * 2**20
        ),
    )(inputs, w_gate, w_up, cotangent)


def solution(mesh):
    nx, ncol, nd = mesh.shape["row"] // 2, mesh.shape["col"], mesh.shape["dp"]
    in_specs = (P("dp", "col", "row"), P("row", "col"), P("row", "col"), P("dp", "row", "col"))
    out_specs = (
        P("dp", "row", "col"),
        P("dp", "col", "row"),
        P("row", ("col", "dp")),
        P("row", ("col", "dp")),
    )
    return jax.shard_map(
        functools.partial(local, nx, ncol, nd), mesh=mesh, in_specs=in_specs, out_specs=out_specs, check_vma=False
    )
```

```python
import functools

import jax
import jax.numpy as jnp
from jax import lax
from jax.experimental import pallas as pl
from jax.experimental.pallas import tpu as pltpu
from jax.sharding import PartitionSpec as P

MESH = pl.DeviceIdType.MESH
F32 = jnp.float32
BF16 = jnp.bfloat16
LANES = 128
PIECES = ((0, 128), (128, 192), (192, 224))
DLAG = 8
VMEM_LIMIT = 53 * 2**20


def wait_bytes(ref, sem):
    pltpu.make_async_copy(ref, ref, sem).wait()


def kernel(
    nx, ny, nd, sub, tb,
    in_ref, wg_ref, wu_ref, cot_ref,
    hid_ref, gi_ref, gg_ref, gu_ref,
    wg, wu, cot, wp, cotp, hidp, everyone, xsend, xrecv, zown, zsend, zrecv, dsend, dall, dfull,
    gsend, gsib, gy, grecv, fsend, frecv, acc, giown,
    hello, loc, agc_s, agc_r, agz_s, agz_r, agy_s, agy_r, agk_s, agk_r, x_s, x_r, z_s, z_r, dz_s, dz_r, dx_s, dx_r,
    gk_s, gk_r, g_s, g_r, f_s, f_r,
):
    row, col, d = lax.axis_index("row"), lax.axis_index("col"), lax.axis_index("dp")
    x, h = row // 2, row % 2
    y, k = col // 2, col % 2
    nz, ncol = 2 * nd, 2 * ny
    z = h * nd + d
    feat = wg.shape[0]
    seven = frecv
    sibling = (row, y * 2 + 1 - k, d)

    def zdev(z2):
        return (x * 2 + z2 // nd, col, z2 % nd)

    def xdev(i):
        return (lax.rem(x + i, nx) * 2 + h, col, d)

    def ydev(i):
        return (row, lax.rem(y + i, ny) * 2 + k, d)

    def cdev(i):
        return (row, lax.rem(col + i, ncol), d)

    def rank(z2):
        return jnp.minimum(z2, nd)

    def send(src, dst, ssem, rsem, dev):
        pltpu.make_async_remote_copy(
            src_ref=src, dst_ref=dst, send_sem=ssem, recv_sem=rsem, device_id=dev, device_id_type=MESH
        ).start()

    barrier = pltpu.get_barrier_semaphore()
    for i in range(1, ncol):
        pl.semaphore_signal(barrier, inc=1, device_id=cdev(i), device_id_type=MESH)
    for i in range(1, nx):
        pl.semaphore_signal(barrier, inc=1, device_id=xdev(i), device_id_type=MESH)
    my_rank = rank(z)
    for i in range(1, nz):
        z2 = lax.rem(z + i, nz)

        @pl.when((rank(z2) > my_rank) | ((h == 1) & (z2 >= nd)))
        def _(z2=z2):
            pl.semaphore_signal(barrier, inc=1, device_id=zdev(z2), device_id_type=MESH)

    loads = [
        pltpu.make_async_copy(wg_ref, wg, loc.at[0]),
        pltpu.make_async_copy(wu_ref, wu, loc.at[1]),
        pltpu.make_async_copy(cot_ref.at[0], cot, loc.at[2]),
        pltpu.make_async_copy(in_ref.at[0], everyone.at[0, y, k], loc.at[3]),
    ]
    for load in loads:
        load.start()
    pl.semaphore_wait(barrier, ncol - 1 + nx - 1 + jnp.where(h == 0, d, nz - 1))

    for i in range(1, ncol):
        send(in_ref.at[0], everyone.at[0, y, k], agc_s, agc_r, cdev(i))
    for i in range(1, nz):
        z2 = lax.rem(z + i, nz)

        @pl.when(rank(z2) < my_rank)
        def _(z2=z2):
            pl.semaphore_signal(hello.at[h], inc=1, device_id=zdev(z2), device_id_type=MESH)

    def gather_z():
        for i in range(1, nd):
            send(in_ref.at[0], everyone.at[i, y, k], agz_s, agz_r.at[i], (row, col, lax.rem(d + i, nd)))

    @pl.when(h == 1)
    def _():
        gather_z()

    for load in loads:
        load.wait()

    @pl.loop(0, feat // 64)
    def _(q):
        rows = pl.ds(pl.multiple_of(q * 64, 64), 64)
        for j in range(nd):
            o = j * sub
            at = 0
            for lo, hi in PIECES:
                for w in (wg, wu):
                    wp[j, rows, at : at + hi - lo] = w[rows, o + lo : o + hi]
                    at += hi - lo
            wp[j, rows, at:] = jnp.zeros((64, 4 * LANES - at), BF16)

    cotp[...] = jnp.zeros_like(cotp)
    half = tb // 2
    for j in range(nd):
        o = j * sub
        cotp[j, :tb, :] = cot[:, o : o + 128]
        cotp[j, tb : 2 * tb, :64] = cot[:, o + 128 : o + 192]
        cotp[j, 2 * tb :, :32] = cot[:half, o + 192 : o + 224]
        cotp[j, 2 * tb :, 64:96] = cot[half:, o + 192 : o + 224]
    acc[...] = jnp.zeros_like(acc)
    wait_bytes(seven.at[pl.ds(0, ncol - 1)], agc_r)

    def stage_a(s):
        j = lax.rem(d + s, nd)
        part = jnp.dot(everyone[0].reshape(ncol * tb, feat), wp[j], preferred_element_type=F32)
        for c in range(3):
            xsend[s, :, c * tb : (c + 1) * tb, :] = (
                part[:, c * LANES : (c + 1) * LANES].reshape(2 * nx, tb, LANES).astype(BF16)
            )
        last = part[:, 3 * LANES :].reshape(2 * nx, 2, half, LANES)
        low, high = last[:, 0].reshape(nx * tb, LANES), last[:, 1].reshape(nx * tb, LANES)
        xsend[s, :, 3 * tb :, :] = (low + pltpu.roll(high, 64, 1)).reshape(2 * nx, half, LANES).astype(BF16)
        for i in range(1, nx):
            other = lax.rem(x + i, nx)
            send(xsend.at[s, pl.ds(other * 2, 2)], xrecv.at[s, i - 1], x_s, x_r.at[s], xdev(i))

    def stage_agz(s):
        @pl.when((h == 0) & (d < nd - 1))
        def _():
            pl.semaphore_wait(hello.at[0], nd - 1 - d)

        @pl.when(h == 0)
        def _():
            gather_z()

    def stage_y(s):
        mine = everyone.at[s, y, k]
        wait_bytes(mine, agz_r.at[s])
        for i in range(1, ny):
            send(mine, mine, agy_s, agy_r.at[s], ydev(i))

    def stage_k(s):
        wait_bytes(everyone.at[s, pl.ds(0, ny - 1), k], agy_r.at[s])
        mine = everyone.at[s, :, k]
        send(mine, mine, agk_s, agk_r.at[s], sibling)

    def stage_b(s):
        wait_bytes(xrecv.at[s], x_r.at[s])

        def total(which):
            out = xsend[s, x * 2 + which].astype(F32)
            for i in range(nx - 1):
                out = out + xrecv[s, i, which].astype(F32)
            return out

        zsend[s] = total(1 - h).astype(BF16)

        @pl.when((s == nd - 1) & (h == 0))
        def _():
            pl.semaphore_wait(hello.at[1], nd)

        send(zsend.at[s], zrecv.at[s], z_s, z_r.at[s], zdev(lax.rem(z + nd, nz)))
        zown[s] = total(h)

    def stage_c(s):
        j = lax.rem(d + s, nd)
        wait_bytes(zrecv.at[s], z_r.at[s])
        both = zown[s] + zrecv[s].astype(F32)
        mid, end = both[2 * tb : 3 * tb], both[3 * tb :]
        gate = jnp.concatenate([both[:tb], mid, end], axis=0)
        upper = jnp.concatenate([both[tb : 2 * tb], pltpu.roll(mid, 64, 1), pltpu.roll(end, 96, 1)], axis=0)
        sig = jax.nn.sigmoid(gate)
        act = gate * sig
        slope = cotp[j].astype(F32)
        hidp[j] = (act * upper).astype(BF16)
        d_gate = slope * upper * sig * (1.0 + gate * (1.0 - sig))
        d_up = slope * act
        dsend[s, :tb, :] = d_gate[:tb].astype(BF16)
        dsend[s, tb : 2 * tb, :] = d_up[:tb].astype(BF16)
        dsend[s, 2 * tb : 3 * tb, :] = (d_gate[tb : 2 * tb] + pltpu.roll(d_up[tb : 2 * tb], 64, 1)).astype(BF16)
        dsend[s, 3 * tb :, :] = (d_gate[2 * tb :] + pltpu.roll(d_up[2 * tb :], 32, 1)).astype(BF16)
        there = dall.at[s, row]

        @pl.when(s == 0)
        def _():
            dall[0, row] = dsend[0]
            send(dsend.at[0], there, dz_s, dz_r.at[s], (x * 2 + 1 - h, col, d))

        @pl.when(s > 0)
        def _():
            send(dsend.at[s], there, dz_s, dz_r.at[s], (x * 2, col, j))
            send(dsend.at[s], there, dz_s, dz_r.at[s], (x * 2 + 1, col, j))

    def stage_d(s):
        @pl.when(s == 0)
        def _():
            wait_bytes(dall.at[0, 0], dz_r.at[0])

        @pl.when(s > 0)
        def _():
            wait_bytes(dall.at[s, pl.ds(0, 2)], dz_r.at[s])

        mine = dall.at[s, pl.ds(x * 2, 2)]
        for i in range(1, nx):
            send(mine, mine, dx_s, dx_r.at[s], xdev(i))

    def stage_e(s):
        wait_bytes(dall.at[s, pl.ds(0, (nx - 1) * 2)], dx_r.at[s])
        for c in range(3):
            dfull[:, c * LANES : (c + 1) * LANES] = dall[s, :, c * tb : (c + 1) * tb, :].reshape(2 * nx * tb, LANES)
        low = dall[s, :, 3 * tb :, :].astype(F32)
        high = pltpu.roll(low.reshape(nx * tb, LANES), 64, 1).reshape(2 * nx, half, LANES)
        dfull[:, 3 * LANES :] = jnp.concatenate([low, high], axis=1).reshape(2 * nx * tb, LANES).astype(BF16)
        part = lax.dot_general(dfull[...], wp[d], (((1,), (1,)), ((), ())), preferred_element_type=F32)
        gsend[s] = part.astype(BF16).reshape(ny, 2, tb, feat)
        send(gsend.at[s, :, 1 - k], gsib.at[s], gk_s, gk_r.at[s], sibling)

        @pl.when(s > 0)
        def _():
            wait_bytes(everyone.at[s, :, k], agk_r.at[s])

        acc[...] += lax.dot_general(
            dfull[...], everyone[s].reshape(ncol * tb, feat), (((0,), (0,)), ((), ())), preferred_element_type=F32
        )

    def stage_f(s):
        wait_bytes(gsib.at[s], gk_r.at[s])
        for i in range(1, ny):
            other = lax.rem(y + i, ny)
            gy[s, i - 1] = (gsend[s, other, k].astype(F32) + gsib[s, other].astype(F32)).astype(BF16)
            send(gy.at[s, i - 1], grecv.at[s, i - 1], g_s, g_r.at[s], ydev(i))

    def stage_h(s):
        wait_bytes(grecv.at[s], g_r.at[s])
        out = gsend[s, y, k].astype(F32) + gsib[s, y].astype(F32)
        for i in range(ny - 1):
            out = out + grecv[s, i].astype(F32)

        @pl.when(s == 0)
        def _():
            giown[...] = out

        @pl.when(s > 0)
        def _():
            fsend[s] = out.astype(BF16)
            send(fsend.at[s], frecv.at[s], f_s, f_r.at[s], (row, col, lax.rem(d - s + nd, nd)))

    def stage_hidden(s):
        for j in range(nd):
            o = j * sub
            hid_ref[0, :, o : o + 128] = hidp[j, :tb, :]
            hid_ref[0, :, o + 128 : o + 192] = hidp[j, tb : 2 * tb, :64]
            hid_ref[0, :half, o + 192 : o + 224] = hidp[j, 2 * tb :, :32]
            hid_ref[0, half:, o + 192 : o + 224] = hidp[j, 2 * tb :, 64:96]

    def stage_weights(s):
        at = 0
        for lo, hi in PIECES:
            for out_ref in (gg_ref, gu_ref):
                out_ref[lo:hi, :] = acc[at : at + hi - lo, :].astype(BF16)
                at += hi - lo

    last = nd - 1
    stages = (
        (stage_a, 0, 0, 2), (stage_a, -1, 3, last), (stage_agz, 1, 0, 0), (stage_b, 1, 0, last), (stage_c, 4, 0, last),
        (stage_y, 5, 0, last - 1), (stage_k, 7, 0, last - 1), (stage_d, DLAG, 0, last), (stage_e, DLAG + 2, 0, last),
        (stage_f, DLAG + 3, 0, last), (stage_h, DLAG + 4, 0, last), (stage_hidden, 13, 0, 0), (stage_weights, DLAG + 10, 0, 0),
    )

    def body(t, carry):
        for fn, lag, low, high in stages:

            @pl.when((t >= lag + low) & (t <= lag + high))
            def _(fn=fn, lag=lag):
                fn(last - (t - lag))

        return carry

    lax.fori_loop(0, nd + DLAG + 4, body, None)

    out = giown[...]
    for s in range(1, nd):
        wait_bytes(frecv.at[s], f_r.at[s])
        out = out + frecv[s].astype(F32)
    gi_ref[0] = out.astype(BF16)

    wait_bytes(seven.at[pl.ds(0, ncol - 1)], agc_s)
    wait_bytes(seven.at[pl.ds(0, nd - 1)], agz_s)
    wait_bytes(everyone.at[pl.ds(0, nd - 1), pl.ds(0, ny - 1), 0], agy_s)
    wait_bytes(everyone.at[pl.ds(0, nd - 1), :, 0], agk_s)
    wait_bytes(xsend.at[:, pl.ds(0, (nx - 1) * 2)], x_s)
    wait_bytes(zsend, z_s)
    wait_bytes(dsend, dz_s)
    wait_bytes(dsend.at[pl.ds(0, nd - 1)], dz_s)
    wait_bytes(dall.at[:, pl.ds(0, (nx - 1) * 2)], dx_s)
    wait_bytes(gsib, gk_s)
    wait_bytes(gy, g_s)
    wait_bytes(fsend.at[pl.ds(0, nd - 1)], f_s)


def local(nx, ny, nd, inputs, w_gate, w_up, cotangent):
    tb, feat = inputs.shape[1], inputs.shape[2]
    ff = w_gate.shape[1]
    sub = ff // nd
    wide = 4 * LANES
    tok = tb * 2 * ny
    rows = tb * 7 // 2
    dma = pltpu.SemaphoreType.DMA
    any_spec = pl.BlockSpec(memory_space=pl.ANY)
    vmem = pl.BlockSpec(memory_space=pltpu.VMEM)
    hidden, grad_inputs, grad_gate, grad_up = pl.pallas_call(
        functools.partial(kernel, nx, ny, nd, sub, tb),
        name="swiglu",
        out_shape=(
            jax.ShapeDtypeStruct((1, tb, ff), BF16),
            jax.ShapeDtypeStruct((1, tb, feat), BF16),
            jax.ShapeDtypeStruct((sub, feat), BF16),
            jax.ShapeDtypeStruct((sub, feat), BF16),
        ),
        in_specs=[any_spec] * 4,
        out_specs=(vmem,) * 4,
        scratch_shapes=[
            pltpu.VMEM((feat, ff), BF16),
            pltpu.VMEM((feat, ff), BF16),
            pltpu.VMEM((tb, ff), BF16),
            pltpu.VMEM((nd, feat, wide), BF16),
            pltpu.VMEM((nd, tb * 5 // 2, LANES), BF16),
            pltpu.VMEM((nd, tb * 5 // 2, LANES), BF16),
            pltpu.VMEM((nd, ny, 2, tb, feat), BF16),
            pltpu.VMEM((nd, 2 * nx, rows, LANES), BF16),
            pltpu.VMEM((nd, nx - 1, 2, rows, LANES), BF16),
            pltpu.VMEM((nd, rows, LANES), F32),
            pltpu.VMEM((nd, rows, LANES), BF16),
            pltpu.VMEM((nd, rows, LANES), BF16),
            pltpu.VMEM((nd, rows, LANES), BF16),
            pltpu.VMEM((nd, 2 * nx, rows, LANES), BF16),
            pltpu.VMEM((tok, wide), BF16),
            pltpu.VMEM((nd, ny, 2, tb, feat), BF16),
            pltpu.VMEM((nd, ny, tb, feat), BF16),
            pltpu.VMEM((nd, ny - 1, tb, feat), BF16),
            pltpu.VMEM((nd, ny - 1, tb, feat), BF16),
            pltpu.VMEM((nd, tb, feat), BF16),
            pltpu.VMEM((nd, tb, feat), BF16),
            pltpu.VMEM((wide, feat), F32),
            pltpu.VMEM((tb, feat), F32),
            pltpu.SemaphoreType.REGULAR((2,)),
            dma((4,)),
            dma, dma,
            dma, dma((nd,)),
            dma, dma((nd,)),
            dma, dma((nd,)),
            dma, dma((nd,)),
            dma, dma((nd,)),
            dma, dma((nd,)),
            dma, dma((nd,)),
            dma, dma((nd,)),
            dma, dma((nd,)),
            dma, dma((nd,)),
        ],
        compiler_params=pltpu.CompilerParams(
            collective_id=0, has_side_effects=True, vmem_limit_bytes=VMEM_LIMIT
        ),
    )(inputs, w_gate, w_up, cotangent)
    return hidden, grad_inputs, grad_gate.T, grad_up.T


def solution(mesh):
    nx, ny, nd = mesh.shape["row"] // 2, mesh.shape["col"] // 2, mesh.shape["dp"]
    in_specs = (P("dp", "col", "row"), P("row", "col"), P("row", "col"), P("dp", "row", "col"))
    out_specs = (
        P("dp", "row", "col"),
        P("dp", "col", "row"),
        P("row", ("col", "dp")),
        P("row", ("col", "dp")),
    )
    return jax.shard_map(
        functools.partial(local, nx, ny, nd), mesh=mesh, in_specs=in_specs, out_specs=out_specs, check_vma=False
    )
```

```python
import functools

import jax
import jax.numpy as jnp
from jax import lax
from jax.experimental import pallas as pl
from jax.experimental.pallas import tpu as pltpu
from jax.sharding import PartitionSpec as P

MESH = pl.DeviceIdType.MESH
F32 = jnp.float32
BF16 = jnp.bfloat16
LANES = 128
PIECES = ((0, 128), (128, 192), (192, 224))
ALEAD, BLEAD, CLAG, C2, YLAG = 1, 0, 4, 0, 8
LAGS = (7, 9, 10, 12)
UPPER = 1
VMEM_LIMIT = 53 * 2**20


def wait_bytes(ref, sem):
    pltpu.make_async_copy(ref, ref, sem).wait()


def kernel(
    nx, ny, nd, sub, tb,
    in_ref, wg_ref, wu_ref, cot_ref,
    hid_ref, gi_ref, gg_ref, gu_ref,
    wg, wu, cot, wp, cotp, hidp, everyone, xsend, xrecv, zown, zsend, zrecv, dsend, dall, dfull,
    gsend, gsib, gy, grecv, fsend, frecv, acc, giown,
    hello, loc, agc_s, agc_r, agz_s, agz_r, agy_s, agy_r, agk_s, agk_r, x_s, x_r, z_s, z_r, dz_s, dz_r, dx_s, dx_r,
    gk_s, gk_r, g_s, g_r, f_s, f_r,
):
    row, col, d = lax.axis_index("row"), lax.axis_index("col"), lax.axis_index("dp")
    x, h = row // 2, row % 2
    y, k = col // 2, col % 2
    nz, ncol = 2 * nd, 2 * ny
    z = h * nd + d
    feat = wg.shape[0]
    seven = frecv
    sibling = (row, y * 2 + 1 - k, d)

    def zdev(z2):
        return (x * 2 + z2 // nd, col, z2 % nd)

    def xdev(i):
        return (lax.rem(x + i, nx) * 2 + h, col, d)

    def ydev(i):
        return (row, lax.rem(y + i, ny) * 2 + k, d)

    def cdev(i):
        return (row, lax.rem(col + i, ncol), d)

    def rank(z2):
        return jnp.minimum(z2, nd)

    def send(src, dst, ssem, rsem, dev):
        pltpu.make_async_remote_copy(
            src_ref=src, dst_ref=dst, send_sem=ssem, recv_sem=rsem, device_id=dev, device_id_type=MESH
        ).start()

    barrier = pltpu.get_barrier_semaphore()
    for i in range(1, ncol):
        pl.semaphore_signal(barrier, inc=1, device_id=cdev(i), device_id_type=MESH)
    for i in range(1, nx):
        pl.semaphore_signal(barrier, inc=1, device_id=xdev(i), device_id_type=MESH)
    my_rank = rank(z)
    for i in range(1, nz):
        z2 = lax.rem(z + i, nz)

        @pl.when((rank(z2) > my_rank) | ((h == 1) & (z2 >= nd)))
        def _(z2=z2):
            pl.semaphore_signal(barrier, inc=1, device_id=zdev(z2), device_id_type=MESH)

    loads = [
        pltpu.make_async_copy(wg_ref, wg, loc.at[0]),
        pltpu.make_async_copy(wu_ref, wu, loc.at[1]),
        pltpu.make_async_copy(cot_ref.at[0], cot, loc.at[2]),
        pltpu.make_async_copy(in_ref.at[0], everyone.at[0, y, k], loc.at[3]),
    ]
    for load in loads:
        load.start()
    pl.semaphore_wait(barrier, ncol - 1 + nx - 1 + jnp.where(h == 0, d, nz - 1))

    for i in range(1, ncol):
        send(in_ref.at[0], everyone.at[0, y, k], agc_s, agc_r, cdev(i))
    for i in range(1, nz):
        z2 = lax.rem(z + i, nz)

        @pl.when(rank(z2) < my_rank)
        def _(z2=z2):
            pl.semaphore_signal(hello.at[h], inc=1, device_id=zdev(z2), device_id_type=MESH)

    def gather_z(when):
        for i in range(1, nd):
            d2 = lax.rem(d + i, nd)
            near = (i == 1) & (d % 2 == 0) | (i == nd - 1) & (d % 2 == 1)

            @pl.when(when(d2))
            def _(i=i, d2=d2):
                send(in_ref.at[0], everyone.at[i, y, k], agz_s, agz_r.at[i], (row, col, d2))

    gather_z(lambda d2: (h == 1) | (d2 < d))

    for load in loads:
        load.wait()

    @pl.loop(0, feat // 64)
    def _(q):
        rows = pl.ds(pl.multiple_of(q * 64, 64), 64)
        for j in range(nd):
            o = j * sub
            at = 0
            for lo, hi in PIECES:
                for w in (wg, wu):
                    wp[j, rows, at : at + hi - lo] = w[rows, o + lo : o + hi]
                    at += hi - lo
            wp[j, rows, at:] = jnp.zeros((64, 4 * LANES - at), BF16)

    cotp[...] = jnp.zeros_like(cotp)
    half = tb // 2
    for j in range(nd):
        o = j * sub
        cotp[j, :tb, :] = cot[:, o : o + 128]
        cotp[j, tb : 2 * tb, :64] = cot[:, o + 128 : o + 192]
        cotp[j, 2 * tb :, :32] = cot[:half, o + 192 : o + 224]
        cotp[j, 2 * tb :, 64:96] = cot[half:, o + 192 : o + 224]
    acc[...] = jnp.zeros_like(acc)
    wait_bytes(seven.at[pl.ds(0, ncol - 1)], agc_r)

    def stage_a(s):
        j = lax.rem(d + s, nd)
        part = jnp.dot(everyone[0].reshape(ncol * tb, feat), wp[j], preferred_element_type=F32)
        for c in range(3):
            xsend[s, :, c * tb : (c + 1) * tb, :] = (
                part[:, c * LANES : (c + 1) * LANES].reshape(2 * nx, tb, LANES).astype(BF16)
            )
        last = part[:, 3 * LANES :].reshape(2 * nx, 2, half, LANES)
        low, high = last[:, 0].reshape(nx * tb, LANES), last[:, 1].reshape(nx * tb, LANES)
        xsend[s, :, 3 * tb :, :] = (low + pltpu.roll(high, 64, 1)).reshape(2 * nx, half, LANES).astype(BF16)
        for i in range(1, nx):
            other = lax.rem(x + i, nx)
            send(xsend.at[s, pl.ds(other * 2, 2)], xrecv.at[s, i - 1], x_s, x_r.at[s], xdev(i))

    def stage_agz(s):
        @pl.when((h == 0) & (d < nd - 1))
        def _():
            pl.semaphore_wait(hello.at[0], nd - 1 - d)
            gather_z(lambda d2: d2 > d)

    def stage_r(s):
        for i in range(2, nd, 2):
            here = everyone.at[i, y, k]
            wait_bytes(here, agz_r.at[i])
            there = i + 1 - 2 * (d % 2)
            send(here, everyone.at[there, y, k], agz_s, agz_r.at[there], (row, col, d + 1 - 2 * (d % 2)))

    def stage_y(s):
        mine = everyone.at[s, y, k]

        wait_bytes(mine, agz_r.at[s])

        for i in range(1, ny):
            send(mine, mine, agy_s, agy_r.at[s], ydev(i))

    def stage_k(s):
        wait_bytes(everyone.at[s, pl.ds(0, ny - 1), k], agy_r.at[s])
        mine = everyone.at[s, :, k]
        send(mine, mine, agk_s, agk_r.at[s], sibling)

    def stage_b(s):
        wait_bytes(xrecv.at[s], x_r.at[s])

        def total(which):
            out = xsend[s, x * 2 + which].astype(F32)
            for i in range(nx - 1):
                out = out + xrecv[s, i, which].astype(F32)
            return out

        zsend[s] = total(1 - h).astype(BF16)

        @pl.when((s == nd - 1) & (h == 0))
        def _():
            pl.semaphore_wait(hello.at[1], nd)

        send(zsend.at[s], zrecv.at[s], z_s, z_r.at[s], zdev(lax.rem(z + nd, nz)))
        zown[s] = total(h)

    def stage_c(s):
        j = lax.rem(d + s, nd)
        wait_bytes(zrecv.at[s], z_r.at[s])
        both = zown[s] + zrecv[s].astype(F32)
        mid, end = both[2 * tb : 3 * tb], both[3 * tb :]
        gate = jnp.concatenate([both[:tb], mid, end], axis=0)
        upper = jnp.concatenate([both[tb : 2 * tb], pltpu.roll(mid, 64, 1), pltpu.roll(end, 96, 1)], axis=0)
        sig = jax.nn.sigmoid(gate)
        act = gate * sig
        slope = cotp[j].astype(F32)
        hidp[j] = (act * upper).astype(BF16)
        d_gate = slope * upper * sig * (1.0 + gate * (1.0 - sig))
        d_up = slope * act
        dsend[s, :tb, :] = d_gate[:tb].astype(BF16)
        dsend[s, tb : 2 * tb, :] = d_up[:tb].astype(BF16)
        dsend[s, 2 * tb : 3 * tb, :] = (d_gate[tb : 2 * tb] + pltpu.roll(d_up[tb : 2 * tb], 64, 1)).astype(BF16)
        dsend[s, 3 * tb :, :] = (d_gate[2 * tb :] + pltpu.roll(d_up[2 * tb :], 32, 1)).astype(BF16)
        there = dall.at[s, row]

        @pl.when(s == 0)
        def _():
            dall[0, row] = dsend[0]

        send_d(s, 0)

    def send_d(s, half_z):
        @pl.when((s > 0) | (h != half_z))
        def _():
            there = dall.at[s, row]
            send(dsend.at[s], there, dz_s, dz_r.at[s], (x * 2 + half_z, col, lax.rem(d + s, nd)))

    def stage_c2(s):
        send_d(s, 1)

    def stage_d(s):
        @pl.when(s == 0)
        def _():
            wait_bytes(dall.at[0, 0], dz_r.at[0])

        @pl.when(s > 0)
        def _():
            wait_bytes(dall.at[s, pl.ds(0, 2)], dz_r.at[s])

        mine = dall.at[s, pl.ds(x * 2, 2)]
        for i in range(1, nx):
            send(mine, mine, dx_s, dx_r.at[s], xdev(i))

    def stage_e(s):
        wait_bytes(dall.at[s, pl.ds(0, (nx - 1) * 2)], dx_r.at[s])
        for c in range(3):
            dfull[s, :, c * LANES : (c + 1) * LANES] = dall[s, :, c * tb : (c + 1) * tb, :].reshape(2 * nx * tb, LANES)
        low = dall[s, :, 3 * tb :, :].astype(F32)
        high = pltpu.roll(low.reshape(nx * tb, LANES), 64, 1).reshape(2 * nx, half, LANES)
        dfull[s, :, 3 * LANES :] = jnp.concatenate([low, high], axis=1).reshape(2 * nx * tb, LANES).astype(BF16)
        part = lax.dot_general(dfull[s], wp[d], (((1,), (1,)), ((), ())), preferred_element_type=F32)
        gsend[s] = part.astype(BF16).reshape(ny, 2, tb, feat)
        send(gsend.at[s, :, 1 - k], gsib.at[s], gk_s, gk_r.at[s], sibling)

    def stage_w(s):
        @pl.when(s > 0)
        def _():
            wait_bytes(everyone.at[s, :, k], agk_r.at[s])

        acc[...] += lax.dot_general(
            dfull[s], everyone[s].reshape(ncol * tb, feat), (((0,), (0,)), ((), ())), preferred_element_type=F32
        )

    def stage_f(s):
        wait_bytes(gsib.at[s], gk_r.at[s])
        for i in range(1, ny):
            other = lax.rem(y + i, ny)
            gy[s, i - 1] = (gsend[s, other, k].astype(F32) + gsib[s, other].astype(F32)).astype(BF16)
            send(gy.at[s, i - 1], grecv.at[s, i - 1], g_s, g_r.at[s], ydev(i))

    def stage_h(s):
        wait_bytes(grecv.at[s], g_r.at[s])
        out = gsend[s, y, k].astype(F32) + gsib[s, y].astype(F32)
        for i in range(ny - 1):
            out = out + grecv[s, i].astype(F32)

        @pl.when(s == 0)
        def _():
            giown[...] = out

        @pl.when(s > 0)
        def _():
            fsend[s] = out.astype(BF16)
            send(fsend.at[s], frecv.at[s], f_s, f_r.at[s], (row, col, lax.rem(d - s + nd, nd)))

    def stage_hidden(s):
        for j in range(nd):
            o = j * sub
            hid_ref[0, :, o : o + 128] = hidp[j, :tb, :]
            hid_ref[0, :, o + 128 : o + 192] = hidp[j, tb : 2 * tb, :64]
            hid_ref[0, :half, o + 192 : o + 224] = hidp[j, 2 * tb :, :32]
            hid_ref[0, half:, o + 192 : o + 224] = hidp[j, 2 * tb :, 64:96]

    def stage_weights(s):
        at = 0
        for lo, hi in PIECES:
            for out_ref in (gg_ref, gu_ref):
                out_ref[lo:hi, :] = acc[at : at + hi - lo, :].astype(BF16)
                at += hi - lo

    last = nd - 1
    late = h * UPPER
    lag_d, lag_e, lag_f, lag_h = (lag + late for lag in LAGS)
    stages = (
        (stage_a, 0, 0, 2), (stage_a, -ALEAD, 3, last), (stage_agz, 1, 0, 0), (stage_b, 1, 0, 2), (stage_b, 1 - BLEAD, 3, last),
        (stage_c, CLAG, 0, last), (stage_c2, CLAG + C2, 0, last), (stage_y, YLAG, 0, last - 1),
        (stage_k, YLAG + 2, 0, last - 1), (stage_d, lag_d, 0, last), (stage_e, lag_e, 0, last),
        (stage_f, lag_f, 0, last), (stage_w, lag_h, 0, last), (stage_weights, lag_h, last, last), (stage_h, lag_h, 0, last),
        (stage_hidden, 13, 0, 0),
    )

    def body(t, carry):
        for fn, lag, low, high in stages:

            @pl.when((t >= lag + low) & (t <= lag + high))
            def _(fn=fn, lag=lag):
                fn(last - (t - lag))

        return carry

    lax.fori_loop(0, nd + LAGS[3] + late, body, None)

    out = giown[...]
    for s in range(1, nd):
        wait_bytes(frecv.at[s], f_r.at[s])
        out = out + frecv[s].astype(F32)
    gi_ref[0] = out.astype(BF16)

    wait_bytes(seven.at[pl.ds(0, ncol - 1)], agc_s)
    wait_bytes(seven.at[pl.ds(0, nd - 1)], agz_s)
    wait_bytes(everyone.at[pl.ds(0, nd - 1), pl.ds(0, ny - 1), 0], agy_s)
    wait_bytes(everyone.at[pl.ds(0, nd - 1), :, 0], agk_s)
    wait_bytes(xsend.at[:, pl.ds(0, (nx - 1) * 2)], x_s)
    wait_bytes(zsend, z_s)
    wait_bytes(dsend, dz_s)
    wait_bytes(dsend.at[pl.ds(0, nd - 1)], dz_s)
    wait_bytes(dall.at[:, pl.ds(0, (nx - 1) * 2)], dx_s)
    wait_bytes(gsib, gk_s)
    wait_bytes(gy, g_s)
    wait_bytes(fsend.at[pl.ds(0, nd - 1)], f_s)


def local(nx, ny, nd, inputs, w_gate, w_up, cotangent):
    tb, feat = inputs.shape[1], inputs.shape[2]
    ff = w_gate.shape[1]
    sub = ff // nd
    wide = 4 * LANES
    tok = tb * 2 * ny
    rows = tb * 7 // 2
    dma = pltpu.SemaphoreType.DMA
    any_spec = pl.BlockSpec(memory_space=pl.ANY)
    vmem = pl.BlockSpec(memory_space=pltpu.VMEM)
    hidden, grad_inputs, grad_gate, grad_up = pl.pallas_call(
        functools.partial(kernel, nx, ny, nd, sub, tb),
        name="swiglu",
        out_shape=(
            jax.ShapeDtypeStruct((1, tb, ff), BF16),
            jax.ShapeDtypeStruct((1, tb, feat), BF16),
            jax.ShapeDtypeStruct((sub, feat), BF16),
            jax.ShapeDtypeStruct((sub, feat), BF16),
        ),
        in_specs=[any_spec] * 4,
        out_specs=(vmem,) * 4,
        scratch_shapes=[
            pltpu.VMEM((feat, ff), BF16),
            pltpu.VMEM((feat, ff), BF16),
            pltpu.VMEM((tb, ff), BF16),
            pltpu.VMEM((nd, feat, wide), BF16),
            pltpu.VMEM((nd, tb * 5 // 2, LANES), BF16),
            pltpu.VMEM((nd, tb * 5 // 2, LANES), BF16),
            pltpu.VMEM((nd, ny, 2, tb, feat), BF16),
            pltpu.VMEM((nd, 2 * nx, rows, LANES), BF16),
            pltpu.VMEM((nd, nx - 1, 2, rows, LANES), BF16),
            pltpu.VMEM((nd, rows, LANES), F32),
            pltpu.VMEM((nd, rows, LANES), BF16),
            pltpu.VMEM((nd, rows, LANES), BF16),
            pltpu.VMEM((nd, rows, LANES), BF16),
            pltpu.VMEM((nd, 2 * nx, rows, LANES), BF16),
            pltpu.VMEM((nd, tok, wide), BF16),
            pltpu.VMEM((nd, ny, 2, tb, feat), BF16),
            pltpu.VMEM((nd, ny, tb, feat), BF16),
            pltpu.VMEM((nd, ny - 1, tb, feat), BF16),
            pltpu.VMEM((nd, ny - 1, tb, feat), BF16),
            pltpu.VMEM((nd, tb, feat), BF16),
            pltpu.VMEM((nd, tb, feat), BF16),
            pltpu.VMEM((wide, feat), F32),
            pltpu.VMEM((tb, feat), F32),
            pltpu.SemaphoreType.REGULAR((2,)),
            dma((4,)),
            dma, dma,
            dma, dma((nd,)),
            dma, dma((nd,)),
            dma, dma((nd,)),
            dma, dma((nd,)),
            dma, dma((nd,)),
            dma, dma((nd,)),
            dma, dma((nd,)),
            dma, dma((nd,)),
            dma, dma((nd,)),
            dma, dma((nd,)),
        ],
        compiler_params=pltpu.CompilerParams(
            collective_id=0, has_side_effects=True, vmem_limit_bytes=VMEM_LIMIT
        ),
    )(inputs, w_gate, w_up, cotangent)
    return hidden, grad_inputs, grad_gate.T, grad_up.T


def solution(mesh):
    nx, ny, nd = mesh.shape["row"] // 2, mesh.shape["col"] // 2, mesh.shape["dp"]
    in_specs = (P("dp", "col", "row"), P("row", "col"), P("row", "col"), P("dp", "row", "col"))
    out_specs = (
        P("dp", "row", "col"),
        P("dp", "col", "row"),
        P("row", ("col", "dp")),
        P("row", ("col", "dp")),
    )
    return jax.shard_map(
        functools.partial(local, nx, ny, nd), mesh=mesh, in_specs=in_specs, out_specs=out_specs, check_vma=False
    )
```

```python
import functools

import jax
import jax.numpy as jnp
from jax import lax
from jax.experimental import pallas as pl
from jax.experimental.pallas import tpu as pltpu
from jax.sharding import PartitionSpec as P

MESH = pl.DeviceIdType.MESH
F32 = jnp.float32
BF16 = jnp.bfloat16
LANES = 128
PIECES = ((0, 128), (128, 192), (192, 224))
ALEAD, BLEAD, CLAG, C2, YLAG = 1, 0, 4, 0, 8
LAGS = (7, 9, 10, 12)
UPPER = 1
VMEM_LIMIT = 53 * 2**20


def wait_bytes(ref, sem):
    pltpu.make_async_copy(ref, ref, sem).wait()


def kernel(
    nx, ny, nd, sub, tb,
    both_ref, wg_ref, wu_ref,
    hid_ref, all_ref,
    wg, wu, cot, wp, cotp, hidp, everyone, xsend, xrecv, zown, zsend, zrecv, dsend, dall, dfull,
    gsend, gsib, gy, grecv, fsend, frecv, acc, giown,
    hello, loc, agc_s, agc_r, agz_s, agz_r, agy_s, agy_r, agk_s, agk_r, x_s, x_r, z_s, z_r, dz_s, dz_r, dx_s, dx_r,
    gk_s, gk_r, g_s, g_r, f_s, f_r,
):
    row, col, d = lax.axis_index("row"), lax.axis_index("col"), lax.axis_index("dp")
    x, h = row // 2, row % 2
    y, k = col // 2, col % 2
    nz, ncol = 2 * nd, 2 * ny
    z = h * nd + d
    feat = wg.shape[0]
    gg_ref, gu_ref = all_ref.at[pl.ds(0, sub)], all_ref.at[pl.ds(sub, sub)]
    ff = wg.shape[1]
    own = both_ref.at[:, pl.ds(ff, feat)]
    seven = frecv
    sibling = (row, y * 2 + 1 - k, d)

    def zdev(z2):
        return (x * 2 + z2 // nd, col, z2 % nd)

    def xdev(i):
        return (lax.rem(x + i, nx) * 2 + h, col, d)

    def ydev(i):
        return (row, lax.rem(y + i, ny) * 2 + k, d)

    def cdev(i):
        return (row, lax.rem(col + i, ncol), d)

    def rank(z2):
        return jnp.minimum(z2, nd)

    def send(src, dst, ssem, rsem, dev):
        pltpu.make_async_remote_copy(
            src_ref=src, dst_ref=dst, send_sem=ssem, recv_sem=rsem, device_id=dev, device_id_type=MESH
        ).start()

    barrier = pltpu.get_barrier_semaphore()
    for i in range(1, ncol):
        pl.semaphore_signal(barrier, inc=1, device_id=cdev(i), device_id_type=MESH)
    for i in range(1, nx):
        pl.semaphore_signal(barrier, inc=1, device_id=xdev(i), device_id_type=MESH)
    my_rank = rank(z)
    for i in range(1, nz):
        z2 = lax.rem(z + i, nz)

        @pl.when((rank(z2) > my_rank) | ((h == 1) & (z2 >= nd)))
        def _(z2=z2):
            pl.semaphore_signal(barrier, inc=1, device_id=zdev(z2), device_id_type=MESH)

    loads = [
        pltpu.make_async_copy(wg_ref, wg, loc.at[0]),
        pltpu.make_async_copy(wu_ref, wu, loc.at[1]),
        pltpu.make_async_copy(both_ref.at[:, pl.ds(0, ff)], cot, loc.at[2]),
        pltpu.make_async_copy(own, everyone.at[0, y, k], loc.at[3]),
    ]
    for load in loads:
        load.start()
    pl.semaphore_wait(barrier, ncol - 1 + nx - 1 + jnp.where(h == 0, d, nz - 1))

    for i in range(1, ncol):
        send(own, everyone.at[0, y, k], agc_s, agc_r, cdev(i))
    for i in range(1, nz):
        z2 = lax.rem(z + i, nz)

        @pl.when(rank(z2) < my_rank)
        def _(z2=z2):
            pl.semaphore_signal(hello.at[h], inc=1, device_id=zdev(z2), device_id_type=MESH)

    def gather_z(when):
        for i in range(1, nd):
            d2 = lax.rem(d + i, nd)
            near = (i == 1) & (d % 2 == 0) | (i == nd - 1) & (d % 2 == 1)

            @pl.when(when(d2))
            def _(i=i, d2=d2):
                send(own, everyone.at[i, y, k], agz_s, agz_r.at[i], (row, col, d2))

    gather_z(lambda d2: (h == 1) | (d2 < d))

    for load in loads:
        load.wait()

    @pl.loop(0, feat // 64)
    def _(q):
        rows = pl.ds(pl.multiple_of(q * 64, 64), 64)
        for j in range(nd):
            o = j * sub
            at = 0
            for lo, hi in PIECES:
                for w in (wg, wu):
                    wp[j, rows, at : at + hi - lo] = w[rows, o + lo : o + hi]
                    at += hi - lo
            wp[j, rows, at:] = jnp.zeros((64, 4 * LANES - at), BF16)

    cotp[...] = jnp.zeros_like(cotp)
    half = tb // 2
    for j in range(nd):
        o = j * sub
        cotp[j, :tb, :] = cot[:, o : o + 128]
        cotp[j, tb : 2 * tb, :64] = cot[:, o + 128 : o + 192]
        cotp[j, 2 * tb :, :32] = cot[:half, o + 192 : o + 224]
        cotp[j, 2 * tb :, 64:96] = cot[half:, o + 192 : o + 224]
    acc[...] = jnp.zeros_like(acc)
    wait_bytes(seven.at[pl.ds(0, ncol - 1)], agc_r)

    def stage_a(s):
        j = lax.rem(d + s, nd)
        part = jnp.dot(everyone[0].reshape(ncol * tb, feat), wp[j], preferred_element_type=F32)
        for c in range(3):
            xsend[s, :, c * tb : (c + 1) * tb, :] = (
                part[:, c * LANES : (c + 1) * LANES].reshape(2 * nx, tb, LANES).astype(BF16)
            )
        last = part[:, 3 * LANES :].reshape(2 * nx, 2, half, LANES)
        low, high = last[:, 0].reshape(nx * tb, LANES), last[:, 1].reshape(nx * tb, LANES)
        xsend[s, :, 3 * tb :, :] = (low + pltpu.roll(high, 64, 1)).reshape(2 * nx, half, LANES).astype(BF16)
        for i in range(1, nx):
            other = lax.rem(x + i, nx)
            send(xsend.at[s, pl.ds(other * 2, 2)], xrecv.at[s, i - 1], x_s, x_r.at[s], xdev(i))

    def stage_agz(s):
        @pl.when((h == 0) & (d < nd - 1))
        def _():
            pl.semaphore_wait(hello.at[0], nd - 1 - d)
            gather_z(lambda d2: d2 > d)

    def stage_r(s):
        for i in range(2, nd, 2):
            here = everyone.at[i, y, k]
            wait_bytes(here, agz_r.at[i])
            there = i + 1 - 2 * (d % 2)
            send(here, everyone.at[there, y, k], agz_s, agz_r.at[there], (row, col, d + 1 - 2 * (d % 2)))

    def stage_y(s):
        mine = everyone.at[s, y, k]

        wait_bytes(mine, agz_r.at[s])

        for i in range(1, ny):
            send(mine, mine, agy_s, agy_r.at[s], ydev(i))

    def stage_k(s):
        wait_bytes(everyone.at[s, pl.ds(0, ny - 1), k], agy_r.at[s])
        mine = everyone.at[s, :, k]
        send(mine, mine, agk_s, agk_r.at[s], sibling)

    def stage_b(s):
        wait_bytes(xrecv.at[s], x_r.at[s])

        def total(which):
            out = xsend[s, x * 2 + which].astype(F32)
            for i in range(nx - 1):
                out = out + xrecv[s, i, which].astype(F32)
            return out

        zsend[s] = total(1 - h).astype(BF16)

        @pl.when((s == nd - 1) & (h == 0))
        def _():
            pl.semaphore_wait(hello.at[1], nd)

        send(zsend.at[s], zrecv.at[s], z_s, z_r.at[s], zdev(lax.rem(z + nd, nz)))
        zown[s] = total(h)

    def stage_c(s):
        j = lax.rem(d + s, nd)
        wait_bytes(zrecv.at[s], z_r.at[s])
        both = zown[s] + zrecv[s].astype(F32)
        mid, end = both[2 * tb : 3 * tb], both[3 * tb :]
        gate = jnp.concatenate([both[:tb], mid, end], axis=0)
        upper = jnp.concatenate([both[tb : 2 * tb], pltpu.roll(mid, 64, 1), pltpu.roll(end, 96, 1)], axis=0)
        sig = jax.nn.sigmoid(gate)
        act = gate * sig
        slope = cotp[j].astype(F32)
        hidp[j] = (act * upper).astype(BF16)
        d_gate = slope * upper * sig * (1.0 + gate * (1.0 - sig))
        d_up = slope * act
        dsend[s, :tb, :] = d_gate[:tb].astype(BF16)
        dsend[s, tb : 2 * tb, :] = d_up[:tb].astype(BF16)
        dsend[s, 2 * tb : 3 * tb, :] = (d_gate[tb : 2 * tb] + pltpu.roll(d_up[tb : 2 * tb], 64, 1)).astype(BF16)
        dsend[s, 3 * tb :, :] = (d_gate[2 * tb :] + pltpu.roll(d_up[2 * tb :], 32, 1)).astype(BF16)
        there = dall.at[s, row]

        @pl.when(s == 0)
        def _():
            dall[0, row] = dsend[0]

        send_d(s, 0)

    def send_d(s, half_z):
        @pl.when((s > 0) | (h != half_z))
        def _():
            there = dall.at[s, row]
            send(dsend.at[s], there, dz_s, dz_r.at[s], (x * 2 + half_z, col, lax.rem(d + s, nd)))

    def stage_c2(s):
        send_d(s, 1)

    def stage_d(s):
        @pl.when(s == 0)
        def _():
            wait_bytes(dall.at[0, 0], dz_r.at[0])

        @pl.when(s > 0)
        def _():
            wait_bytes(dall.at[s, pl.ds(0, 2)], dz_r.at[s])

        mine = dall.at[s, pl.ds(x * 2, 2)]
        for i in range(1, nx):
            send(mine, mine, dx_s, dx_r.at[s], xdev(i))

    def stage_e(s):
        wait_bytes(dall.at[s, pl.ds(0, (nx - 1) * 2)], dx_r.at[s])
        for c in range(3):
            dfull[s, :, c * LANES : (c + 1) * LANES] = dall[s, :, c * tb : (c + 1) * tb, :].reshape(2 * nx * tb, LANES)
        low = dall[s, :, 3 * tb :, :].astype(F32)
        high = pltpu.roll(low.reshape(nx * tb, LANES), 64, 1).reshape(2 * nx, half, LANES)
        dfull[s, :, 3 * LANES :] = jnp.concatenate([low, high], axis=1).reshape(2 * nx * tb, LANES).astype(BF16)
        part = lax.dot_general(dfull[s], wp[d], (((1,), (1,)), ((), ())), preferred_element_type=F32)
        gsend[s] = part.astype(BF16).reshape(ny, 2, tb, feat)
        send(gsend.at[s, :, 1 - k], gsib.at[s], gk_s, gk_r.at[s], sibling)

    def stage_w(s):
        @pl.when(s > 0)
        def _():
            wait_bytes(everyone.at[s, :, k], agk_r.at[s])

        acc[...] += lax.dot_general(
            dfull[s], everyone[s].reshape(ncol * tb, feat), (((0,), (0,)), ((), ())), preferred_element_type=F32
        )

    def stage_f(s):
        wait_bytes(gsib.at[s], gk_r.at[s])
        for i in range(1, ny):
            other = lax.rem(y + i, ny)
            gy[s, i - 1] = (gsend[s, other, k].astype(F32) + gsib[s, other].astype(F32)).astype(BF16)
            send(gy.at[s, i - 1], grecv.at[s, i - 1], g_s, g_r.at[s], ydev(i))

    def stage_h(s):
        wait_bytes(grecv.at[s], g_r.at[s])
        out = gsend[s, y, k].astype(F32) + gsib[s, y].astype(F32)
        for i in range(ny - 1):
            out = out + grecv[s, i].astype(F32)

        @pl.when(s == 0)
        def _():
            giown[...] = out

        @pl.when(s > 0)
        def _():
            fsend[s] = out.astype(BF16)
            send(fsend.at[s], frecv.at[s], f_s, f_r.at[s], (row, col, lax.rem(d - s + nd, nd)))

    def stage_hidden(s):
        for j in range(nd):
            o = j * sub
            hid_ref[0, :, o : o + 128] = hidp[j, :tb, :]
            hid_ref[0, :, o + 128 : o + 192] = hidp[j, tb : 2 * tb, :64]
            hid_ref[0, :half, o + 192 : o + 224] = hidp[j, 2 * tb :, :32]
            hid_ref[0, half:, o + 192 : o + 224] = hidp[j, 2 * tb :, 64:96]

    def stage_weights(s):
        at = 0
        for lo, hi in PIECES:
            for out_ref in (gg_ref, gu_ref):
                out_ref[lo:hi, :] = acc[at : at + hi - lo, :].astype(BF16)
                at += hi - lo

    last = nd - 1
    late = h * UPPER
    lag_d, lag_e, lag_f, lag_h = (lag + late for lag in LAGS)
    stages = (
        (stage_a, 0, 0, 2), (stage_a, -ALEAD, 3, last), (stage_agz, 1, 0, 0), (stage_b, 1, 0, 2), (stage_b, 1 - BLEAD, 3, last),
        (stage_y, YLAG, 0, last - 1),
        (stage_k, YLAG + 2, 0, last - 1), (stage_d, lag_d, 0, last), (stage_c, CLAG, 0, last), (stage_c2, CLAG + C2, 0, last), (stage_e, lag_e, 0, last),
        (stage_f, lag_f, 0, last), (stage_w, lag_h, 0, last), (stage_weights, lag_h, last, last), (stage_h, lag_h, 0, last),
        (stage_hidden, 13, 0, 0),
    )

    def body(t, carry):
        for fn, lag, low, high in stages:

            @pl.when((t >= lag + low) & (t <= lag + high))
            def _(fn=fn, lag=lag):
                fn(last - (t - lag))

        return carry

    lax.fori_loop(0, nd + LAGS[3] + late, body, None)

    out = giown[...]
    for s in range(1, nd):
        wait_bytes(frecv.at[s], f_r.at[s])
        out = out + frecv[s].astype(F32)
    all_ref[2 * sub :] = out.astype(BF16)

    wait_bytes(seven.at[pl.ds(0, ncol - 1)], agc_s)
    wait_bytes(seven.at[pl.ds(0, nd - 1)], agz_s)
    wait_bytes(everyone.at[pl.ds(0, nd - 1), pl.ds(0, ny - 1), 0], agy_s)
    wait_bytes(everyone.at[pl.ds(0, nd - 1), :, 0], agk_s)
    wait_bytes(xsend.at[:, pl.ds(0, (nx - 1) * 2)], x_s)
    wait_bytes(zsend, z_s)
    wait_bytes(dsend, dz_s)
    wait_bytes(dsend.at[pl.ds(0, nd - 1)], dz_s)
    wait_bytes(dall.at[:, pl.ds(0, (nx - 1) * 2)], dx_s)
    wait_bytes(gsib, gk_s)
    wait_bytes(gy, g_s)
    wait_bytes(fsend.at[pl.ds(0, nd - 1)], f_s)


def local(nx, ny, nd, inputs, w_gate, w_up, cotangent):
    tb, feat = inputs.shape[1], inputs.shape[2]
    ff = w_gate.shape[1]
    sub = ff // nd
    wide = 4 * LANES
    tok = tb * 2 * ny
    rows = tb * 7 // 2
    dma = pltpu.SemaphoreType.DMA
    any_spec = pl.BlockSpec(memory_space=pl.ANY)
    vmem = pl.BlockSpec(memory_space=pltpu.VMEM)
    hidden, others = pl.pallas_call(
        functools.partial(kernel, nx, ny, nd, sub, tb),
        name="swiglu",
        out_shape=(
            jax.ShapeDtypeStruct((1, tb, ff), BF16),
            jax.ShapeDtypeStruct((2 * sub + tb, feat), BF16),
        ),
        in_specs=[any_spec] * 3,
        out_specs=(vmem,) * 2,
        scratch_shapes=[
            pltpu.VMEM((feat, ff), BF16),
            pltpu.VMEM((feat, ff), BF16),
            pltpu.VMEM((tb, ff), BF16),
            pltpu.VMEM((nd, feat, wide), BF16),
            pltpu.VMEM((nd, tb * 5 // 2, LANES), BF16),
            pltpu.VMEM((nd, tb * 5 // 2, LANES), BF16),
            pltpu.VMEM((nd, ny, 2, tb, feat), BF16),
            pltpu.VMEM((nd, 2 * nx, rows, LANES), BF16),
            pltpu.VMEM((nd, nx - 1, 2, rows, LANES), BF16),
            pltpu.VMEM((nd, rows, LANES), F32),
            pltpu.VMEM((nd, rows, LANES), BF16),
            pltpu.VMEM((nd, rows, LANES), BF16),
            pltpu.VMEM((nd, rows, LANES), BF16),
            pltpu.VMEM((nd, 2 * nx, rows, LANES), BF16),
            pltpu.VMEM((nd, tok, wide), BF16),
            pltpu.VMEM((nd, ny, 2, tb, feat), BF16),
            pltpu.VMEM((nd, ny, tb, feat), BF16),
            pltpu.VMEM((nd, ny - 1, tb, feat), BF16),
            pltpu.VMEM((nd, ny - 1, tb, feat), BF16),
            pltpu.VMEM((nd, tb, feat), BF16),
            pltpu.VMEM((nd, tb, feat), BF16),
            pltpu.VMEM((wide, feat), F32),
            pltpu.VMEM((tb, feat), F32),
            pltpu.SemaphoreType.REGULAR((2,)),
            dma((4,)),
            dma, dma,
            dma, dma((nd,)),
            dma, dma((nd,)),
            dma, dma((nd,)),
            dma, dma((nd,)),
            dma, dma((nd,)),
            dma, dma((nd,)),
            dma, dma((nd,)),
            dma, dma((nd,)),
            dma, dma((nd,)),
            dma, dma((nd,)),
        ],
        compiler_params=pltpu.CompilerParams(
            collective_id=0, has_side_effects=True, vmem_limit_bytes=VMEM_LIMIT
        ),
    )(jnp.concatenate([cotangent[0], inputs[0]], axis=1), w_gate, w_up)
    return hidden, others[None, 2 * sub :], others[:sub].T, others[sub : 2 * sub].T


def solution(mesh):
    nx, ny, nd = mesh.shape["row"] // 2, mesh.shape["col"] // 2, mesh.shape["dp"]
    in_specs = (P("dp", "col", "row"), P("row", "col"), P("row", "col"), P("dp", "row", "col"))
    out_specs = (
        P("dp", "row", "col"),
        P("dp", "col", "row"),
        P("row", ("col", "dp")),
        P("row", ("col", "dp")),
    )
    return jax.shard_map(
        functools.partial(local, nx, ny, nd), mesh=mesh, in_specs=in_specs, out_specs=out_specs, check_vma=False
    )
```

```python
import functools

import jax
import jax.numpy as jnp
from jax import lax
from jax.experimental import pallas as pl
from jax.experimental.pallas import tpu as pltpu
from jax.sharding import PartitionSpec as P

MESH = pl.DeviceIdType.MESH
F32 = jnp.float32
BF16 = jnp.bfloat16
LANES = 128
PIECES = ((0, 128), (128, 192), (192, 224))
ALEAD, BLEAD, CLAG, C2, YLAG = 1, 0, 4, 0, 8
LAGS = (7, 9, 10, 12)
UPPER = 1
VMEM_LIMIT = 53 * 2**20


def wait_bytes(ref, sem):
    pltpu.make_async_copy(ref, ref, sem).wait()


def kernel(
    nx, ny, nd, sub, tb,
    both_ref, wg_ref, wu_ref,
    hid_ref, all_ref,
    wg, wu, cot, wp, cotp, hidp, everyone, xsend, xrecv, zown, zsend, zrecv, dsend, dall, dfull,
    gsend, gsib, gy, grecv, fsend, frecv, acc, giown,
    hello, loc, agc_s, agc_r, agz_s, agz_r, agy_s, agy_r, agk_s, agk_r, x_s, x_r, z_s, z_r, dz_s, dz_r, dx_s, dx_r,
    gk_s, gk_r, g_s, g_r, f_s, f_r,
):
    row, col, d = lax.axis_index("row"), lax.axis_index("col"), lax.axis_index("dp")
    x, h = row // 2, row % 2
    y, k = col // 2, col % 2
    nz, ncol = 2 * nd, 2 * ny
    z = h * nd + d
    feat = wg.shape[0]
    gg_ref, gu_ref = all_ref.at[pl.ds(0, sub)], all_ref.at[pl.ds(sub, sub)]
    ff = wg.shape[1]
    own = both_ref.at[:, pl.ds(ff, feat)]
    seven = frecv
    sibling = (row, y * 2 + 1 - k, d)

    def zdev(z2):
        return (x * 2 + z2 // nd, col, z2 % nd)

    def xdev(i):
        return (lax.rem(x + i, nx) * 2 + h, col, d)

    def ydev(i):
        return (row, lax.rem(y + i, ny) * 2 + k, d)

    def cdev(i):
        return (row, lax.rem(col + i, ncol), d)

    def rank(z2):
        return jnp.minimum(z2, nd)

    def send(src, dst, ssem, rsem, dev):
        pltpu.make_async_remote_copy(
            src_ref=src, dst_ref=dst, send_sem=ssem, recv_sem=rsem, device_id=dev, device_id_type=MESH
        ).start()

    barrier = pltpu.get_barrier_semaphore()
    for i in range(1, ncol):
        pl.semaphore_signal(barrier, inc=1, device_id=cdev(i), device_id_type=MESH)
    for i in range(1, nx):
        pl.semaphore_signal(barrier, inc=1, device_id=xdev(i), device_id_type=MESH)
    my_rank = rank(z)
    for i in range(1, nz):
        z2 = lax.rem(z + i, nz)

        @pl.when((rank(z2) > my_rank) | ((h == 1) & (z2 >= nd)))
        def _(z2=z2):
            pl.semaphore_signal(barrier, inc=1, device_id=zdev(z2), device_id_type=MESH)

    loads = [
        pltpu.make_async_copy(wg_ref, wg, loc.at[0]),
        pltpu.make_async_copy(wu_ref, wu, loc.at[1]),
        pltpu.make_async_copy(both_ref.at[:, pl.ds(0, ff)], cot, loc.at[2]),
        pltpu.make_async_copy(own, everyone.at[0, y, k], loc.at[3]),
    ]
    for load in loads:
        load.start()
    pl.semaphore_wait(barrier, ncol - 1 + nx - 1 + jnp.where(h == 0, d, nz - 1))

    for i in sorted(range(1, ncol), key=lambda i: abs(i - ncol // 2)):
        send(own, everyone.at[0, y, k], agc_s, agc_r, cdev(i))
    for i in range(1, nz):
        z2 = lax.rem(z + i, nz)

        @pl.when(rank(z2) < my_rank)
        def _(z2=z2):
            pl.semaphore_signal(hello.at[h], inc=1, device_id=zdev(z2), device_id_type=MESH)

    def gather_z(when):
        for i in range(1, nd):
            d2 = lax.rem(d + i, nd)
            near = (i == 1) & (d % 2 == 0) | (i == nd - 1) & (d % 2 == 1)

            @pl.when(when(d2))
            def _(i=i, d2=d2):
                send(own, everyone.at[i, y, k], agz_s, agz_r.at[i], (row, col, d2))

    gather_z(lambda d2: (h == 1) | (d2 < d))

    for load in loads:
        load.wait()

    @pl.loop(0, feat // 64)
    def _(q):
        rows = pl.ds(pl.multiple_of(q * 64, 64), 64)
        for j in range(nd):
            o = j * sub
            at = 0
            for lo, hi in PIECES:
                for w in (wg, wu):
                    wp[j, rows, at : at + hi - lo] = w[rows, o + lo : o + hi]
                    at += hi - lo
            wp[j, rows, at:] = jnp.zeros((64, 4 * LANES - at), BF16)

    cotp[...] = jnp.zeros_like(cotp)
    half = tb // 2
    for j in range(nd):
        o = j * sub
        cotp[j, :tb, :] = cot[:, o : o + 128]
        cotp[j, tb : 2 * tb, :64] = cot[:, o + 128 : o + 192]
        cotp[j, 2 * tb :, :32] = cot[:half, o + 192 : o + 224]
        cotp[j, 2 * tb :, 64:96] = cot[half:, o + 192 : o + 224]
    acc[...] = jnp.zeros_like(acc)
    wait_bytes(seven.at[pl.ds(0, ncol - 1)], agc_r)

    def stage_a(s):
        j = lax.rem(d + s, nd)
        part = jnp.dot(everyone[0].reshape(ncol * tb, feat), wp[j], preferred_element_type=F32)
        for c in range(3):
            xsend[s, :, c * tb : (c + 1) * tb, :] = (
                part[:, c * LANES : (c + 1) * LANES].reshape(2 * nx, tb, LANES).astype(BF16)
            )
        last = part[:, 3 * LANES :].reshape(2 * nx, 2, half, LANES)
        low, high = last[:, 0].reshape(nx * tb, LANES), last[:, 1].reshape(nx * tb, LANES)
        xsend[s, :, 3 * tb :, :] = (low + pltpu.roll(high, 64, 1)).reshape(2 * nx, half, LANES).astype(BF16)
        for i in range(1, nx):
            other = lax.rem(x + i, nx)
            send(xsend.at[s, pl.ds(other * 2, 2)], xrecv.at[s, i - 1], x_s, x_r.at[s], xdev(i))

    def stage_agz(s):
        @pl.when((h == 0) & (d < nd - 1))
        def _():
            pl.semaphore_wait(hello.at[0], nd - 1 - d)
            gather_z(lambda d2: d2 > d)

    def stage_r(s):
        for i in range(2, nd, 2):
            here = everyone.at[i, y, k]
            wait_bytes(here, agz_r.at[i])
            there = i + 1 - 2 * (d % 2)
            send(here, everyone.at[there, y, k], agz_s, agz_r.at[there], (row, col, d + 1 - 2 * (d % 2)))

    def stage_y(s):
        mine = everyone.at[s, y, k]

        wait_bytes(mine, agz_r.at[s])

        for i in range(1, ny):
            send(mine, mine, agy_s, agy_r.at[s], ydev(i))

    def stage_k(s):
        wait_bytes(everyone.at[s, pl.ds(0, ny - 1), k], agy_r.at[s])
        mine = everyone.at[s, :, k]
        send(mine, mine, agk_s, agk_r.at[s], sibling)

    def stage_b(s):
        wait_bytes(xrecv.at[s], x_r.at[s])

        def total(which):
            out = xsend[s, x * 2 + which].astype(F32)
            for i in range(nx - 1):
                out = out + xrecv[s, i, which].astype(F32)
            return out

        zsend[s] = total(1 - h).astype(BF16)

        @pl.when((s == nd - 1) & (h == 0))
        def _():
            pl.semaphore_wait(hello.at[1], nd)

        send(zsend.at[s], zrecv.at[s], z_s, z_r.at[s], zdev(lax.rem(z + nd, nz)))
        zown[s] = total(h)

    def stage_c(s):
        j = lax.rem(d + s, nd)
        wait_bytes(zrecv.at[s], z_r.at[s])
        both = zown[s] + zrecv[s].astype(F32)
        mid, end = both[2 * tb : 3 * tb], both[3 * tb :]
        gate = jnp.concatenate([both[:tb], mid, end], axis=0)
        upper = jnp.concatenate([both[tb : 2 * tb], pltpu.roll(mid, 64, 1), pltpu.roll(end, 96, 1)], axis=0)
        sig = jax.nn.sigmoid(gate)
        act = gate * sig
        slope = cotp[j].astype(F32)
        hidp[j] = (act * upper).astype(BF16)
        d_gate = slope * upper * sig * (1.0 + gate * (1.0 - sig))
        d_up = slope * act
        dsend[s, :tb, :] = d_gate[:tb].astype(BF16)
        dsend[s, tb : 2 * tb, :] = d_up[:tb].astype(BF16)
        dsend[s, 2 * tb : 3 * tb, :] = (d_gate[tb : 2 * tb] + pltpu.roll(d_up[tb : 2 * tb], 64, 1)).astype(BF16)
        dsend[s, 3 * tb :, :] = (d_gate[2 * tb :] + pltpu.roll(d_up[2 * tb :], 32, 1)).astype(BF16)
        there = dall.at[s, row]

        @pl.when(s == 0)
        def _():
            dall[0, row] = dsend[0]

        send_d(s, 0)

    def send_d(s, half_z):
        @pl.when((s > 0) | (h != half_z))
        def _():
            there = dall.at[s, row]
            send(dsend.at[s], there, dz_s, dz_r.at[s], (x * 2 + half_z, col, lax.rem(d + s, nd)))

    def stage_c2(s):
        send_d(s, 1)

    def stage_d(s):
        @pl.when(s == 0)
        def _():
            wait_bytes(dall.at[0, 0], dz_r.at[0])

        @pl.when(s > 0)
        def _():
            wait_bytes(dall.at[s, pl.ds(0, 2)], dz_r.at[s])

        mine = dall.at[s, pl.ds(x * 2, 2)]
        for i in range(1, nx):
            send(mine, mine, dx_s, dx_r.at[s], xdev(i))

    def stage_e(s):
        wait_bytes(dall.at[s, pl.ds(0, (nx - 1) * 2)], dx_r.at[s])
        for c in range(3):
            dfull[s, :, c * LANES : (c + 1) * LANES] = dall[s, :, c * tb : (c + 1) * tb, :].reshape(2 * nx * tb, LANES)
        low = dall[s, :, 3 * tb :, :].astype(F32)
        high = pltpu.roll(low.reshape(nx * tb, LANES), 64, 1).reshape(2 * nx, half, LANES)
        dfull[s, :, 3 * LANES :] = jnp.concatenate([low, high], axis=1).reshape(2 * nx * tb, LANES).astype(BF16)
        part = lax.dot_general(dfull[s], wp[d], (((1,), (1,)), ((), ())), preferred_element_type=F32)
        gsend[s] = part.astype(BF16).reshape(ny, 2, tb, feat)
        send(gsend.at[s, :, 1 - k], gsib.at[s], gk_s, gk_r.at[s], sibling)

    def stage_w(s):
        @pl.when(s > 0)
        def _():
            wait_bytes(everyone.at[s, :, k], agk_r.at[s])

        acc[...] += lax.dot_general(
            dfull[s], everyone[s].reshape(ncol * tb, feat), (((0,), (0,)), ((), ())), preferred_element_type=F32
        )

    def stage_f(s):
        wait_bytes(gsib.at[s], gk_r.at[s])
        for i in range(1, ny):
            other = lax.rem(y + i, ny)
            gy[s, i - 1] = (gsend[s, other, k].astype(F32) + gsib[s, other].astype(F32)).astype(BF16)
            send(gy.at[s, i - 1], grecv.at[s, i - 1], g_s, g_r.at[s], ydev(i))

    def stage_h(s):
        wait_bytes(grecv.at[s], g_r.at[s])
        out = gsend[s, y, k].astype(F32) + gsib[s, y].astype(F32)
        for i in range(ny - 1):
            out = out + grecv[s, i].astype(F32)

        @pl.when(s == 0)
        def _():
            giown[...] = out

        @pl.when(s > 0)
        def _():
            fsend[s] = out.astype(BF16)
            send(fsend.at[s], frecv.at[s], f_s, f_r.at[s], (row, col, lax.rem(d - s + nd, nd)))

    def stage_hidden(s):
        for j in range(nd):
            o = j * sub
            hid_ref[0, :, o : o + 128] = hidp[j, :tb, :]
            hid_ref[0, :, o + 128 : o + 192] = hidp[j, tb : 2 * tb, :64]
            hid_ref[0, :half, o + 192 : o + 224] = hidp[j, 2 * tb :, :32]
            hid_ref[0, half:, o + 192 : o + 224] = hidp[j, 2 * tb :, 64:96]

    def stage_weights(s):
        at = 0
        for lo, hi in PIECES:
            for out_ref in (gg_ref, gu_ref):
                out_ref[lo:hi, :] = acc[at : at + hi - lo, :].astype(BF16)
                at += hi - lo

    last = nd - 1
    late = h * UPPER
    lag_d, lag_e, lag_f, lag_h = (lag + late for lag in LAGS)
    stages = (
        (stage_a, 0, 0, 2), (stage_a, -ALEAD, 3, last), (stage_agz, 1, 0, 0), (stage_b, 1, 0, 2), (stage_b, 1 - BLEAD, 3, last),
        (stage_y, YLAG, 0, last - 1),
        (stage_k, YLAG + 2, 0, last - 1), (stage_d, lag_d, 0, last), (stage_c, CLAG, 0, last), (stage_c2, CLAG + C2, 0, last), (stage_e, lag_e, 0, last),
        (stage_f, lag_f, 0, last), (stage_w, lag_h, 0, last), (stage_weights, lag_h, last, last), (stage_h, lag_h, 0, last),
        (stage_hidden, 13, 0, 0),
    )

    def body(t, carry):
        for fn, lag, low, high in stages:

            @pl.when((t >= lag + low) & (t <= lag + high))
            def _(fn=fn, lag=lag):
                fn(last - (t - lag))

        return carry

    lax.fori_loop(0, nd + LAGS[3] + late, body, None)

    out = giown[...]
    for s in range(1, nd):
        wait_bytes(frecv.at[s], f_r.at[s])
        out = out + frecv[s].astype(F32)
    all_ref[2 * sub :] = out.astype(BF16)

    wait_bytes(seven.at[pl.ds(0, ncol - 1)], agc_s)
    wait_bytes(seven.at[pl.ds(0, nd - 1)], agz_s)
    wait_bytes(everyone.at[pl.ds(0, nd - 1), pl.ds(0, ny - 1), 0], agy_s)
    wait_bytes(everyone.at[pl.ds(0, nd - 1), :, 0], agk_s)
    wait_bytes(xsend.at[:, pl.ds(0, (nx - 1) * 2)], x_s)
    wait_bytes(zsend, z_s)
    wait_bytes(dsend, dz_s)
    wait_bytes(dsend.at[pl.ds(0, nd - 1)], dz_s)
    wait_bytes(dall.at[:, pl.ds(0, (nx - 1) * 2)], dx_s)
    wait_bytes(gsib, gk_s)
    wait_bytes(gy, g_s)
    wait_bytes(fsend.at[pl.ds(0, nd - 1)], f_s)


def local(nx, ny, nd, inputs, w_gate, w_up, cotangent):
    tb, feat = inputs.shape[1], inputs.shape[2]
    ff = w_gate.shape[1]
    sub = ff // nd
    wide = 4 * LANES
    tok = tb * 2 * ny
    rows = tb * 7 // 2
    dma = pltpu.SemaphoreType.DMA
    any_spec = pl.BlockSpec(memory_space=pl.ANY)
    vmem = pl.BlockSpec(memory_space=pltpu.VMEM)
    hidden, others = pl.pallas_call(
        functools.partial(kernel, nx, ny, nd, sub, tb),
        name="swiglu",
        out_shape=(
            jax.ShapeDtypeStruct((1, tb, ff), BF16),
            jax.ShapeDtypeStruct((2 * sub + tb, feat), BF16),
        ),
        in_specs=[any_spec] * 3,
        out_specs=(vmem,) * 2,
        scratch_shapes=[
            pltpu.VMEM((feat, ff), BF16),
            pltpu.VMEM((feat, ff), BF16),
            pltpu.VMEM((tb, ff), BF16),
            pltpu.VMEM((nd, feat, wide), BF16),
            pltpu.VMEM((nd, tb * 5 // 2, LANES), BF16),
            pltpu.VMEM((nd, tb * 5 // 2, LANES), BF16),
            pltpu.VMEM((nd, ny, 2, tb, feat), BF16),
            pltpu.VMEM((nd, 2 * nx, rows, LANES), BF16),
            pltpu.VMEM((nd, nx - 1, 2, rows, LANES), BF16),
            pltpu.VMEM((nd, rows, LANES), F32),
            pltpu.VMEM((nd, rows, LANES), BF16),
            pltpu.VMEM((nd, rows, LANES), BF16),
            pltpu.VMEM((nd, rows, LANES), BF16),
            pltpu.VMEM((nd, 2 * nx, rows, LANES), BF16),
            pltpu.VMEM((nd, tok, wide), BF16),
            pltpu.VMEM((nd, ny, 2, tb, feat), BF16),
            pltpu.VMEM((nd, ny, tb, feat), BF16),
            pltpu.VMEM((nd, ny - 1, tb, feat), BF16),
            pltpu.VMEM((nd, ny - 1, tb, feat), BF16),
            pltpu.VMEM((nd, tb, feat), BF16),
            pltpu.VMEM((nd, tb, feat), BF16),
            pltpu.VMEM((wide, feat), F32),
            pltpu.VMEM((tb, feat), F32),
            pltpu.SemaphoreType.REGULAR((2,)),
            dma((4,)),
            dma, dma,
            dma, dma((nd,)),
            dma, dma((nd,)),
            dma, dma((nd,)),
            dma, dma((nd,)),
            dma, dma((nd,)),
            dma, dma((nd,)),
            dma, dma((nd,)),
            dma, dma((nd,)),
            dma, dma((nd,)),
            dma, dma((nd,)),
        ],
        compiler_params=pltpu.CompilerParams(
            collective_id=0, has_side_effects=True, vmem_limit_bytes=VMEM_LIMIT
        ),
    )(jnp.concatenate([cotangent[0], inputs[0]], axis=1), w_gate, w_up)
    return hidden, others[None, 2 * sub :], others[:sub].T, others[sub : 2 * sub].T


def solution(mesh):
    nx, ny, nd = mesh.shape["row"] // 2, mesh.shape["col"] // 2, mesh.shape["dp"]
    in_specs = (P("dp", "col", "row"), P("row", "col"), P("row", "col"), P("dp", "row", "col"))
    out_specs = (
        P("dp", "row", "col"),
        P("dp", "col", "row"),
        P("row", ("col", "dp")),
        P("row", ("col", "dp")),
    )
    return jax.shard_map(
        functools.partial(local, nx, ny, nd), mesh=mesh, in_specs=in_specs, out_specs=out_specs, check_vma=False
    )
```
